32 devices in a mesh: grp: 2 (over y), blk: 8 (over z, x), seq: 2 (over core).
Axes of the slice: x: 2, y: 2, z: 4, core: 2. Of those that a mesh axis runs over, the one named last changes fastest.
Arguments:
- image_qkv: bfloat16 [4096, 4608], P(('grp', 'blk', 'seq')), parts along dimension 0, may hold values from -6 to 6
- image_qkv_tangent: bfloat16 [4096, 4608], P(('grp', 'blk', 'seq')), parts along dimension 0, may hold values from -6 to 6
- text_kv: bfloat16 [1024, 3072], P(('grp', 'blk', 'seq')), parts along dimension 0, may hold values from -6 to 6
- text_kv_tangent: bfloat16 [1024, 3072], P(('grp', 'blk', 'seq')), parts along dimension 0, may hold values from -6 to 6
- out_weight: bfloat16 [1536, 3072], P(None, ('blk', 'seq')), may hold values from -0.15625 to 0.15625
- gate_table: float32 [64, 3072], replicated, may hold values from -6 to 6
- timesteps: int32 [16], P(('grp', 'blk')), parts along dimension 0, may hold values from 0 to 63
- image_lengths: int32 [16], P(('grp', 'blk')), parts along dimension 0, may hold values from 128 to 256, as said below
- text_lengths: int32 [16], P(('grp', 'blk')), parts along dimension 0, may hold values from 16 to 64, as said below
Outputs:
- output: bfloat16 [4096, 3072], P(('grp', 'blk', 'seq')), parts along dimension 0
- output_tangent: bfloat16 [4096, 3072], P(('grp', 'blk', 'seq')), parts along dimension 0
The draws below stay inside these ranges and needn't reach their ends.
There are 2 independent parts, one for each index of `grp`. The reference program is written for one: setup_inputs(seed, part) draws one part's arguments, and reference() takes and returns one part's arrays. A program takes and returns all parts, laid end to end along the dimension named above; an argument that names none is the same for every part. Nothing has to cross between parts.
Inputs may be any that keep to these rules, and one draw needn't show every extreme that they name: `image_lengths`: the first that many of an image's 256 image slots are live; some image has all of them live. `text_lengths`: the first that many of an image's 64 text slots are live; some image has all of them live.
All inputs are finite; a program needn't handle non-finite values.
Results may differ from the reference program's by a relative error of at most 0.0059.
Values may be sent and summed in bfloat16 or wider, within the bound.
A program may use at most 128 MiB of HBM per device.

```python
import jax
import jax.numpy as jnp
from jax import lax

D = 3072
HS = 128
HEADS = 12
STEPS = 64
IMG_SLOTS = 256
TXT_SLOTS = 64
IMAGES = 8


def draw_image_qkv(key, part):
    key = jax.random.fold_in(key, 11)
    first_key = jax.random.fold_in(key, 0)
    full_shape = (IMAGES, IMG_SLOTS, 3, HEADS, HS)
    scales = jnp.array([2.0, 1.0, 1.0], jnp.float32).reshape(1, 1, 3, 1, 1)
    planted = jnp.clip(jax.random.normal(first_key, full_shape, jnp.float32), -3.0, 3.0) * scales
    return planted.reshape(IMAGES * IMG_SLOTS, 3 * HEADS * HS).astype(jnp.bfloat16)


def draw_image_lengths(key, part):
    key = jax.random.fold_in(key, 21)
    first_key, second_key = jax.random.split(key)
    lengths = jax.random.randint(first_key, (IMAGES,), IMG_SLOTS // 2, IMG_SLOTS + 1)
    full_image = jax.random.randint(second_key, (), 0, IMAGES)
    return jnp.where(jnp.arange(IMAGES) == full_image, IMG_SLOTS, lengths).astype(jnp.int32)


def draw_text_lengths(key, part):
    key = jax.random.fold_in(key, 31)
    first_key, second_key = jax.random.split(key)
    lengths = jax.random.randint(first_key, (IMAGES,), max(1, TXT_SLOTS // 4), TXT_SLOTS + 1)
    full_image = jax.random.randint(second_key, (), 0, IMAGES)
    return jnp.where(jnp.arange(IMAGES) == full_image, TXT_SLOTS, lengths).astype(jnp.int32)


def set_ends(values, rng, least, high):
    shape = values.shape
    spot = [jax.random.randint(jax.random.fold_in(rng, axis), (), 0, shape[axis]) for axis in range(len(shape))]
    values = values.at[tuple(spot)].set(least)
    longest = shape.index(max(shape))
    spot[longest] = (spot[longest] + 1) % shape[longest]
    return values.at[tuple(spot)].set(high)


def level_of(stream_key, shape, pieces, least, high):
    level = 1.0
    for axis_at, blocks in pieces:
        draws = jax.random.uniform(jax.random.fold_in(jax.random.fold_in(stream_key, 6), axis_at), (blocks,), jnp.float32, least / len(pieces), high / len(pieces))
        level = level * jnp.repeat(jnp.exp(draws), shape[axis_at] // blocks).reshape((-1,) + (1,) * (len(shape) - 1 - axis_at))
    return level


def normal_values(rng, shape, deviation, reach, shards=(), held_as=jnp.bfloat16):
    result = deviation * jax.random.normal(rng, shape, jnp.float32)
    if shards:
        result = result * level_of(rng, shape, shards, -0.22, 0.18)
    return jnp.clip(result, -reach, reach).astype(held_as)


def setup_inputs(seed: int = 0, part: int = 0) -> dict:
    key_list = jax.random.split(jax.random.key(seed), 10)
    part_keys = jax.random.split(jax.random.fold_in(key_list[9], part), 10)
    image_qkv = draw_image_qkv(jax.random.fold_in(jax.random.fold_in(key_list[9], part), 71), part)
    image_qkv_tangent = normal_values(part_keys[1], (IMAGES * IMG_SLOTS, 3 * HEADS * HS), 1.0, 6.0, ((0, 16),))
    text_kv = normal_values(part_keys[2], (IMAGES * TXT_SLOTS, 2 * HEADS * HS), 1.0, 6.0, ((0, 16),))
    text_kv_tangent = normal_values(part_keys[3], (IMAGES * TXT_SLOTS, 2 * HEADS * HS), 1.0, 6.0, ((0, 16),))
    out_weight = normal_values(key_list[4], (HEADS * HS, D), (HEADS * HS) ** -0.5, 0.15625, ((1, 16),))
    gate_table = normal_values(key_list[5], (STEPS, D), 1.0, 6.0, (), jnp.float32)
    timesteps = set_ends(jax.random.randint(part_keys[6], (IMAGES,), 0, STEPS), jax.random.fold_in(part_keys[6], 1), 0, STEPS - 1).astype(jnp.int32)
    image_lengths = draw_image_lengths(jax.random.fold_in(jax.random.fold_in(key_list[9], part), 71), part)
    text_lengths = draw_text_lengths(jax.random.fold_in(jax.random.fold_in(key_list[9], part), 71), part)
    return {"image_qkv": image_qkv, "image_qkv_tangent": image_qkv_tangent, "text_kv": text_kv, "text_kv_tangent": text_kv_tangent, "out_weight": out_weight, "gate_table": gate_table, "timesteps": timesteps, "image_lengths": image_lengths, "text_lengths": text_lengths}


def attend(queries, tangent_queries, all_keys, tangent_keys, all_values, tangent_values, usable):
    factor = HS ** -0.5
    queries32 = queries.astype(jnp.float32)
    keys32 = all_keys.astype(jnp.float32)
    scores = jnp.einsum("qhd,khd->hqk", queries32, keys32) * factor
    tangent_scores = (jnp.einsum("qhd,khd->hqk", tangent_queries.astype(jnp.float32), keys32)
                      + jnp.einsum("qhd,khd->hqk", queries32, tangent_keys.astype(jnp.float32))) * factor
    masked = jnp.where(usable[None, None, :], scores, -1e30)
    highest = jnp.max(masked, axis=-1, keepdims=True)
    raised = jnp.where(usable[None, None, :], jnp.exp(masked - highest), 0.0)
    weights = raised / jnp.sum(raised, axis=-1, keepdims=True)
    probs = lax.optimization_barrier(weights.astype(jnp.bfloat16)).astype(jnp.float32)
    centred = tangent_scores - jnp.sum(weights * tangent_scores, axis=-1, keepdims=True)
    tangent_probs = lax.optimization_barrier((weights * centred).astype(jnp.bfloat16)).astype(jnp.float32)
    values32 = all_values.astype(jnp.float32)
    attended = jnp.einsum("hqk,khd->qhd", probs, values32)
    tangent_attended = (jnp.einsum("hqk,khd->qhd", tangent_probs, values32)
                        + jnp.einsum("hqk,khd->qhd", probs, tangent_values.astype(jnp.float32)))
    return attended.astype(jnp.bfloat16), tangent_attended.astype(jnp.bfloat16)


def reference(image_qkv, image_qkv_tangent, text_kv, text_kv_tangent, out_weight, gate_table, timesteps, image_lengths, text_lengths):
    image_primal = image_qkv.reshape(IMAGES, IMG_SLOTS, 3, HEADS, HS)
    image_tangent = image_qkv_tangent.reshape(IMAGES, IMG_SLOTS, 3, HEADS, HS)
    text_primal = text_kv.reshape(IMAGES, TXT_SLOTS, 2, HEADS, HS)
    text_tangent = text_kv_tangent.reshape(IMAGES, TXT_SLOTS, 2, HEADS, HS)

    def one_image(inputs):
        primal, tangent, text_part, text_tan, image_count, text_count = inputs
        all_keys = jnp.concatenate([text_part[:, 0], primal[:, 1]], axis=0)
        tangent_keys = jnp.concatenate([text_tan[:, 0], tangent[:, 1]], axis=0)
        all_values = jnp.concatenate([text_part[:, 1], primal[:, 2]], axis=0)
        tangent_values = jnp.concatenate([text_tan[:, 1], tangent[:, 2]], axis=0)
        text_slots = jnp.arange(TXT_SLOTS, dtype=jnp.int32)
        image_slots = jnp.arange(IMG_SLOTS, dtype=jnp.int32)
        usable = jnp.concatenate([text_slots < text_count, image_slots < image_count], axis=0)
        return attend(primal[:, 0], tangent[:, 0], all_keys, tangent_keys, all_values, tangent_values, usable)

    attended, tangent_attended = lax.map(one_image, (image_primal, image_tangent, text_primal, text_tangent, image_lengths, text_lengths))
    flat = attended.reshape(IMAGES * IMG_SLOTS, HEADS * HS)
    flat_tangent = tangent_attended.reshape(IMAGES * IMG_SLOTS, HEADS * HS)
    gates = jnp.repeat(gate_table[timesteps], IMG_SLOTS, axis=0)
    output = (jnp.dot(flat, out_weight, preferred_element_type=jnp.float32) * gates).astype(jnp.bfloat16)
    output_tangent = (jnp.dot(flat_tangent, out_weight, preferred_element_type=jnp.float32) * gates).astype(jnp.bfloat16)
    return output, output_tangent
```

```python
import jax
import jax.numpy as jnp
from jax import lax
from jax.experimental import pallas as pl
from jax.experimental.pallas import tpu as pltpu
from jax.sharding import PartitionSpec as P

HS = 128
HEADS = 12


def attend(queries, tangent_queries, all_keys, tangent_keys, all_values, tangent_values, usable):
    factor = HS ** (-0.5)
    scores = (
        jnp.einsum("qhd,khd->hqk", queries, all_keys, preferred_element_type=jnp.float32) * factor
    )
    tangent_scores = (
        jnp.einsum("qhd,khd->hqk", tangent_queries, all_keys, preferred_element_type=jnp.float32)
        + jnp.einsum("qhd,khd->hqk", queries, tangent_keys, preferred_element_type=jnp.float32)
    ) * factor
    masked = jnp.where(usable[None, None, :], scores, -1e30)
    highest = jnp.max(masked, axis=-1, keepdims=True)
    raised = jnp.where(usable[None, None, :], jnp.exp(masked - highest), 0.0)
    weights = raised / jnp.sum(raised, axis=-1, keepdims=True)
    probs = weights.astype(jnp.bfloat16)
    centred = tangent_scores - jnp.sum(weights * tangent_scores, axis=-1, keepdims=True)
    tangent_probs = (weights * centred).astype(jnp.bfloat16)
    attended = jnp.einsum("hqk,khd->qhd", probs, all_values, preferred_element_type=jnp.float32)
    tangent_attended = jnp.einsum(
        "hqk,khd->qhd", tangent_probs, all_values, preferred_element_type=jnp.float32
    ) + jnp.einsum("hqk,khd->qhd", probs, tangent_values, preferred_element_type=jnp.float32)
    return (attended.astype(jnp.bfloat16), tangent_attended.astype(jnp.bfloat16))


def column_projector(stacked_rows, shard_piece):
    return jnp.dot(stacked_rows, shard_piece, preferred_element_type=jnp.float32)


def body(
    image_qkv,
    image_qkv_tangent,
    text_kv,
    text_kv_tangent,
    out_weight,
    gate_table,
    timesteps,
    image_lengths,
    text_lengths,
):
    row_count = image_qkv.shape[0]
    text_count = text_kv.shape[0]
    seq_count = lax.axis_size("seq")
    local_heads = HEADS // seq_count
    image_primal = image_qkv.reshape(row_count, 3, seq_count, local_heads, HS)
    image_tangent = image_qkv_tangent.reshape(row_count, 3, seq_count, local_heads, HS)
    text_primal = text_kv.reshape(text_count, 2, seq_count, local_heads, HS)
    text_tangent = text_kv_tangent.reshape(text_count, 2, seq_count, local_heads, HS)
    image_live = image_lengths[0]
    text_live = text_lengths[0]
    primal = lax.all_to_all(image_primal, "seq", split_axis=2, concat_axis=0, tiled=True)[:, :, 0]
    tangent = lax.all_to_all(image_tangent, "seq", split_axis=2, concat_axis=0, tiled=True)[:, :, 0]
    text_part = lax.all_to_all(text_primal, "seq", split_axis=2, concat_axis=0, tiled=True)[:, :, 0]
    text_tan = lax.all_to_all(text_tangent, "seq", split_axis=2, concat_axis=0, tiled=True)[:, :, 0]
    usable = jnp.concatenate(
        [
            jnp.arange(text_part.shape[0], dtype=jnp.int32) < text_live,
            jnp.arange(primal.shape[0], dtype=jnp.int32) < image_live,
        ],
        axis=0,
    )
    all_keys = jnp.concatenate([text_part[:, 0], primal[:, 1]], axis=0)
    tangent_keys = jnp.concatenate([text_tan[:, 0], tangent[:, 1]], axis=0)
    all_values = jnp.concatenate([text_part[:, 1], primal[:, 2]], axis=0)
    tangent_values = jnp.concatenate([text_tan[:, 1], tangent[:, 2]], axis=0)
    attended, tangent_attended = attend(
        primal[:, 0], tangent[:, 0], all_keys, tangent_keys, all_values, tangent_values, usable
    )
    gate_row = lax.dynamic_index_in_dim(gate_table, timesteps[0], 0, keepdims=False)
    local_primal, local_tangent = (
        lax.all_to_all(attended, "seq", split_axis=0, concat_axis=1, tiled=True),
        lax.all_to_all(tangent_attended, "seq", split_axis=0, concat_axis=1, tiled=True),
    )
    stacked_rows = jnp.concatenate(
        [local_primal.reshape(row_count, HEADS * HS), local_tangent.reshape(row_count, HEADS * HS)],
        axis=0,
    )
    projected = column_projector(
        stacked_rows, lax.all_gather(out_weight, ("blk", "seq"), axis=1, tiled=True)
    )
    output = (projected[:row_count] * gate_row).astype(jnp.bfloat16)
    output_tangent = (projected[row_count:] * gate_row).astype(jnp.bfloat16)
    return (output, output_tangent)


MESH = pl.DeviceIdType.MESH
DEPTH = 4
QUARTERS = 4
LAST = 13
UP, DOWN, ACROSS, SIDE, CORE = 0, 1, 2, 3, 4


def fused_kernel(
    lengths,
    shard,
    image_qkv,
    image_tan,
    text_kv,
    text_tan,
    gate,
    out,
    out_tan,
    weights,
    queries,
    keyvals,
    attended,
    send_sem,
    recv_sem,
    core_sem,
    pair_send,
    pair_recv,
    local_sem,
):
    side = lax.axis_index("grp")
    blk = lax.axis_index("blk")
    core = lax.axis_index("seq")
    plane, across = blk // 2, blk % 2
    mate = 1 - core
    width = HEADS * HS
    rows = image_qkv.shape[0]
    texts = text_kv.shape[0]
    own_text, own_image = 2 * texts, 2 * texts + rows

    def target(way):
        if way == UP:
            return (side, blk + 2, core)
        if way == DOWN:
            return (side, blk - 2, core)
        if way == ACROSS:
            return (side, plane * 2 + (1 - across), core)
        if way == SIDE:
            return (1 - side, blk, core)
        return (side, blk, mate)

    locals_ = [pltpu.make_async_copy(shard, weights.at[blk, core], local_sem.at[0])]
    for part, (image, text) in enumerate(((image_qkv, text_kv), (image_tan, text_tan))):
        locals_.append(
            pltpu.make_async_copy(
                image.at[:, pl.ds(0, width)], queries.at[part], local_sem.at[1 + 3 * part]
            )
        )
        locals_.append(
            pltpu.make_async_copy(
                text, keyvals.at[part, pl.ds(0, texts)], local_sem.at[2 + 3 * part]
            )
        )
        locals_.append(
            pltpu.make_async_copy(
                image.at[:, pl.ds(width, 2 * width)],
                keyvals.at[part, pl.ds(own_text, rows)],
                local_sem.at[3 + 3 * part],
            )
        )
    for copy in locals_:
        copy.start()

    barrier = pltpu.get_barrier_semaphore()
    for way in (ACROSS, SIDE, CORE):
        pl.semaphore_signal(barrier, inc=1, device_id=target(way), device_id_type=MESH)

    @pl.when(plane < DEPTH - 1)
    def _():
        pl.semaphore_signal(barrier, inc=1, device_id=target(UP), device_id_type=MESH)

    @pl.when(plane > 0)
    def _():
        pl.semaphore_signal(barrier, inc=1, device_id=target(DOWN), device_id_type=MESH)

    ends = (plane == 0).astype(jnp.int32) + (plane == DEPTH - 1).astype(jnp.int32)
    pl.semaphore_wait(barrier, 5 - ends)
    locals_[0].wait()

    def send(block, piece, way):
        place = weights.at[block, core, piece]
        arrived = core_sem if way == CORE else recv_sem
        return pltpu.make_async_remote_copy(
            src_ref=place,
            dst_ref=place,
            send_sem=send_sem.at[block, piece, way],
            recv_sem=arrived.at[block, piece],
            device_id=target(way),
            device_id_type=MESH,
        )

    def arrival(block, piece):
        send(block, piece, ACROSS).wait_recv()

    def mate_arrival(block, piece):
        place = weights.at[block, mate, piece]
        pltpu.make_async_remote_copy(
            src_ref=place,
            dst_ref=place,
            send_sem=send_sem.at[block, piece, CORE],
            recv_sem=core_sem.at[block, piece],
            device_id=target(CORE),
            device_id_type=MESH,
        ).wait_recv()

    def quarter(k):
        return (k + 2 * side) % QUARTERS

    other = plane * 2 + (1 - across)

    def block_at(at, flip):
        return at * 2 + (across + flip) % 2

    def both_lines(block, piece, act):
        @pl.when(plane < DEPTH - 1)
        def _():
            act(send(block, piece, UP))

        @pl.when(plane > 0)
        def _():
            act(send(block, piece, DOWN))

    def own_sends(act):
        for k in range(QUARTERS):
            piece = quarter(k)
            if k < 2:
                both_lines(blk, piece, act)
            act(send(blk, piece, ACROSS))
        for k in range(QUARTERS):
            act(send(blk, quarter(k), CORE))

    def stage(j, wait, act):
        @pl.when(j < QUARTERS)
        def _():
            piece = quarter(j)
            wait(other, piece)

            @pl.when(j == 0)
            def _():
                both_lines(other, piece, act)

            act(send(other, piece, CORE))

        @pl.when(j < 3 * (DEPTH - 1))
        def _():
            step, item = j // 3 + 1, j % 3
            flip, piece = item // 2, quarter(item % 2)
            for way, at in ((UP, plane - step), (DOWN, plane + step)):

                @pl.when((at >= 0) & (at < DEPTH))
                def _():
                    block = block_at(at, flip)
                    wait(block, piece)
                    more = plane < DEPTH - 1 if way == UP else plane > 0

                    @pl.when(more)
                    def _():
                        act(send(block, piece, way))

                    act(send(block, piece, SIDE))

                    @pl.when(item == 1)
                    def _():
                        act(send(block, piece, ACROSS))

                    act(send(block, piece, CORE))

        late = j - 2

        @pl.when((late >= 0) & (late < 3 * (DEPTH - 1)))
        def _():
            step, item = (j + 1) // 3, (j + 1) % 3
            flip, piece = item // 2, quarter(item % 2 + 2)
            for at in (plane - step, plane + step):

                @pl.when((at >= 0) & (at < DEPTH))
                def _():
                    block = block_at(at, flip)
                    wait(block, piece)

                    @pl.when(item == 1)
                    def _():
                        act(send(block, piece, ACROSS))

                    act(send(block, piece, CORE))

        @pl.when((j >= 4) & (j < 4 + 3 * (DEPTH - 1)) & ((j + 2) % 3 == 1))
        def _():
            step = (j + 2) // 3 - 1
            for at in (plane - step, plane + step):

                @pl.when((at >= 0) & (at < DEPTH))
                def _():
                    block = block_at(at, 1)
                    for k in (1, 3):
                        piece = quarter(k)
                        wait(block, piece)
                        act(send(block, piece, CORE))

    pair = []
    for part, (image, text) in enumerate(((image_qkv, text_kv), (image_tan, text_tan))):
        for nth, (source, place) in enumerate(
            (
                (text, keyvals.at[part, pl.ds(texts, texts)]),
                (image.at[:, pl.ds(width, 2 * width)], keyvals.at[part, pl.ds(own_image, rows)]),
            )
        ):
            pair.append(
                pltpu.make_async_remote_copy(
                    src_ref=source,
                    dst_ref=place,
                    send_sem=pair_send.at[2 * part + nth],
                    recv_sem=pair_recv.at[2 * part + nth],
                    device_id=target(CORE),
                    device_id_type=MESH,
                )
            )
    for copy in pair:
        copy.start()
    own_sends(lambda copy: copy.start())
    for copy in locals_[1:]:
        copy.wait()
    for copy in pair:
        copy.wait()

    image_live, text_live = lengths[0], lengths[1]
    count = 2 * (texts + rows)
    slot = lax.broadcasted_iota(jnp.int32, (1, count), 1)
    text_at = slot + jnp.where(slot < texts, core * texts, mate * texts - texts)
    image_at = slot - own_text + jnp.where(slot < own_image, core * rows, mate * rows - rows)
    position = jnp.where(slot < own_text, text_at, image_at)
    room = jnp.where(slot < own_text, text_live, image_live) - position

    def one_head(head):
        factor = HS ** (-0.5)
        lanes = pl.ds(pl.multiple_of(head * HS, HS), HS)
        value_lanes = pl.ds(pl.multiple_of(width + head * HS, HS), HS)
        q, dq = queries[0, :, lanes], queries[1, :, lanes]
        k, dk = keyvals[0, :, lanes], keyvals[1, :, lanes]
        v, dv = keyvals[0, :, value_lanes], keyvals[1, :, value_lanes]
        nt = (((1,), (1,)), ((), ()))
        scores = lax.dot_general(q, k, nt, preferred_element_type=jnp.float32) * factor
        tangent = (
            lax.dot_general(
                jnp.concatenate([dq, q], axis=1),
                jnp.concatenate([k, dk], axis=1),
                nt,
                preferred_element_type=jnp.float32,
            )
            * factor
        )
        usable = jnp.broadcast_to(room, scores.shape) > 0
        masked = jnp.where(usable, scores, -1e30)
        highest = jnp.max(masked, axis=-1, keepdims=True)
        raised = jnp.where(usable, jnp.exp(masked - highest), 0.0)
        weight = raised * (1.0 / jnp.sum(raised, axis=-1, keepdims=True))
        probs = weight.astype(jnp.bfloat16)
        product = weight * tangent
        mean = jnp.sum(product, axis=-1, keepdims=True)
        tangent_probs = (product - weight * mean).astype(jnp.bfloat16)
        both = jnp.dot(
            probs, jnp.concatenate([v, dv], axis=1), preferred_element_type=jnp.float32
        )
        moved = jnp.dot(tangent_probs, v, preferred_element_type=jnp.float32)
        attended[pl.ds(0, rows), lanes] = both[:, :HS].astype(jnp.bfloat16)
        attended[pl.ds(rows, rows), lanes] = (moved + both[:, HS:]).astype(jnp.bfloat16)

    def project(block):
        for k in range(QUARTERS):
            mate_arrival(block, k)
        share = weights[block]
        size = 2 * shard.shape[0] * shard.shape[1]
        columns = pl.ds(pl.multiple_of(block * size, 128), size)
        made = lax.dot_general(
            attended[...],
            share.reshape(size, width),
            (((1,), (1,)), ((), ())),
            preferred_element_type=jnp.float32,
        )
        made = (made * gate[:, columns]).astype(jnp.bfloat16)
        out[:, columns] = made[:rows]
        out_tan[:, columns] = made[rows:]

    def loop(j, carry):
        stage(j, arrival, lambda copy: copy.start())

        @pl.when(j < HEADS // 2)
        def _():
            one_head(2 * j)
            one_head(2 * j + 1)

        @pl.when(j >= HEADS // 2)
        def _():
            nth = j - HEADS // 2
            at = plane + (1 - 2 * (nth % 2)) * ((nth + 1) // 2)

            @pl.when((at >= 0) & (at < DEPTH))
            def _():
                def one(flip, carry):
                    project(block_at(at, flip))
                    return carry

                lax.fori_loop(0, 2, one, 0)

        return carry

    lax.fori_loop(0, LAST, loop, 0)

    own_sends(lambda copy: copy.wait_send())

    def drain(j, carry):
        stage(j, lambda block, piece: None, lambda copy: copy.wait_send())
        return carry

    lax.fori_loop(0, LAST, drain, 0)


def fused_body(
    image_qkv,
    image_qkv_tangent,
    text_kv,
    text_kv_tangent,
    out_weight,
    gate_table,
    timesteps,
    image_lengths,
    text_lengths,
):
    rows, texts = image_qkv.shape[0], text_kv.shape[0]
    width, share = out_weight.shape
    blocks = lax.axis_size("blk")
    features = gate_table.shape[1]
    shard = out_weight.T.reshape(QUARTERS, share // QUARTERS, width)
    gate_row = lax.dynamic_index_in_dim(gate_table, timesteps[0], 0, keepdims=True)
    lengths = jnp.concatenate([image_lengths, text_lengths])
    whole = pl.BlockSpec(memory_space=pl.ANY)
    vmem = pl.BlockSpec(memory_space=pltpu.VMEM)
    made = jax.ShapeDtypeStruct((rows, features), jnp.bfloat16)
    return tuple(
        pl.pallas_call(
            fused_kernel,
            out_shape=(made, made),
            in_specs=[pl.BlockSpec(memory_space=pltpu.SMEM)] + [whole] * 5 + [vmem],
            out_specs=(vmem, vmem),
            scratch_shapes=[
                pltpu.VMEM((blocks, 2, QUARTERS, share // QUARTERS, width), jnp.bfloat16),
                pltpu.VMEM((2, rows, width), jnp.bfloat16),
                pltpu.VMEM((2, 2 * (rows + texts), 2 * width), jnp.bfloat16),
                pltpu.VMEM((2 * rows, width), jnp.bfloat16),
                pltpu.SemaphoreType.DMA((blocks, QUARTERS, 5)),
                pltpu.SemaphoreType.DMA((blocks, QUARTERS)),
                pltpu.SemaphoreType.DMA((blocks, QUARTERS)),
                pltpu.SemaphoreType.DMA((4,)),
                pltpu.SemaphoreType.DMA((4,)),
                pltpu.SemaphoreType.DMA((7,)),
            ],
            compiler_params=pltpu.CompilerParams(
                collective_id=0, has_side_effects=True, vmem_limit_bytes=44 * 1024 * 1024
            ),
        )(lengths, shard, image_qkv, image_qkv_tangent, text_kv, text_kv_tangent, gate_row)
    )


def fits(mesh):
    sizes = dict(mesh.shape)
    return sizes["grp"] == 2 and sizes["seq"] == 2 and sizes["blk"] == 2 * DEPTH


def solution(mesh):
    in_specs = (
        P(("grp", "blk", "seq"), None),
        P(("grp", "blk", "seq"), None),
        P(("grp", "blk", "seq"), None),
        P(("grp", "blk", "seq"), None),
        P(None, ("blk", "seq")),
        P(),
        P(("grp", "blk")),
        P(("grp", "blk")),
        P(("grp", "blk")),
    )
    out_specs = (P(("grp", "blk", "seq"), None), P(("grp", "blk", "seq"), None))
    chosen = fused_body if fits(mesh) else body
    return jax.shard_map(chosen, mesh=mesh, in_specs=in_specs, out_specs=out_specs, check_vma=False)
```

```python
import jax
import jax.numpy as jnp
from jax import lax
from jax.experimental import pallas as pl
from jax.experimental.pallas import tpu as pltpu
from jax.sharding import PartitionSpec as P

HS = 128
HEADS = 12


def attend(queries, tangent_queries, all_keys, tangent_keys, all_values, tangent_values, usable):
    factor = HS ** (-0.5)
    scores = (
        jnp.einsum("qhd,khd->hqk", queries, all_keys, preferred_element_type=jnp.float32) * factor
    )
    tangent_scores = (
        jnp.einsum("qhd,khd->hqk", tangent_queries, all_keys, preferred_element_type=jnp.float32)
        + jnp.einsum("qhd,khd->hqk", queries, tangent_keys, preferred_element_type=jnp.float32)
    ) * factor
    masked = jnp.where(usable[None, None, :], scores, -1e30)
    highest = jnp.max(masked, axis=-1, keepdims=True)
    raised = jnp.where(usable[None, None, :], jnp.exp(masked - highest), 0.0)
    weights = raised / jnp.sum(raised, axis=-1, keepdims=True)
    probs = weights.astype(jnp.bfloat16)
    centred = tangent_scores - jnp.sum(weights * tangent_scores, axis=-1, keepdims=True)
    tangent_probs = (weights * centred).astype(jnp.bfloat16)
    attended = jnp.einsum("hqk,khd->qhd", probs, all_values, preferred_element_type=jnp.float32)
    tangent_attended = jnp.einsum(
        "hqk,khd->qhd", tangent_probs, all_values, preferred_element_type=jnp.float32
    ) + jnp.einsum("hqk,khd->qhd", probs, tangent_values, preferred_element_type=jnp.float32)
    return (attended.astype(jnp.bfloat16), tangent_attended.astype(jnp.bfloat16))


def column_projector(stacked_rows, shard_piece):
    return jnp.dot(stacked_rows, shard_piece, preferred_element_type=jnp.float32)


def body(
    image_qkv,
    image_qkv_tangent,
    text_kv,
    text_kv_tangent,
    out_weight,
    gate_table,
    timesteps,
    image_lengths,
    text_lengths,
):
    row_count = image_qkv.shape[0]
    text_count = text_kv.shape[0]
    seq_count = lax.axis_size("seq")
    local_heads = HEADS // seq_count
    image_primal = image_qkv.reshape(row_count, 3, seq_count, local_heads, HS)
    image_tangent = image_qkv_tangent.reshape(row_count, 3, seq_count, local_heads, HS)
    text_primal = text_kv.reshape(text_count, 2, seq_count, local_heads, HS)
    text_tangent = text_kv_tangent.reshape(text_count, 2, seq_count, local_heads, HS)
    image_live = image_lengths[0]
    text_live = text_lengths[0]
    primal = lax.all_to_all(image_primal, "seq", split_axis=2, concat_axis=0, tiled=True)[:, :, 0]
    tangent = lax.all_to_all(image_tangent, "seq", split_axis=2, concat_axis=0, tiled=True)[:, :, 0]
    text_part = lax.all_to_all(text_primal, "seq", split_axis=2, concat_axis=0, tiled=True)[:, :, 0]
    text_tan = lax.all_to_all(text_tangent, "seq", split_axis=2, concat_axis=0, tiled=True)[:, :, 0]
    usable = jnp.concatenate(
        [
            jnp.arange(text_part.shape[0], dtype=jnp.int32) < text_live,
            jnp.arange(primal.shape[0], dtype=jnp.int32) < image_live,
        ],
        axis=0,
    )
    all_keys = jnp.concatenate([text_part[:, 0], primal[:, 1]], axis=0)
    tangent_keys = jnp.concatenate([text_tan[:, 0], tangent[:, 1]], axis=0)
    all_values = jnp.concatenate([text_part[:, 1], primal[:, 2]], axis=0)
    tangent_values = jnp.concatenate([text_tan[:, 1], tangent[:, 2]], axis=0)
    attended, tangent_attended = attend(
        primal[:, 0], tangent[:, 0], all_keys, tangent_keys, all_values, tangent_values, usable
    )
    gate_row = lax.dynamic_index_in_dim(gate_table, timesteps[0], 0, keepdims=False)
    local_primal, local_tangent = (
        lax.all_to_all(attended, "seq", split_axis=0, concat_axis=1, tiled=True),
        lax.all_to_all(tangent_attended, "seq", split_axis=0, concat_axis=1, tiled=True),
    )
    stacked_rows = jnp.concatenate(
        [local_primal.reshape(row_count, HEADS * HS), local_tangent.reshape(row_count, HEADS * HS)],
        axis=0,
    )
    projected = column_projector(
        stacked_rows, lax.all_gather(out_weight, ("blk", "seq"), axis=1, tiled=True)
    )
    output = (projected[:row_count] * gate_row).astype(jnp.bfloat16)
    output_tangent = (projected[row_count:] * gate_row).astype(jnp.bfloat16)
    return (output, output_tangent)


MESH = pl.DeviceIdType.MESH
DEPTH = 4
QUARTERS = 4
LAST = 13
LAG = 4
UP, DOWN, ACROSS, SIDE, CORE = 0, 1, 2, 3, 4


def fused_kernel(
    timesteps,
    image_lengths,
    text_lengths,
    shard,
    image_qkv,
    image_tan,
    text_kv,
    text_tan,
    gate_table,
    out,
    out_tan,
    weights,
    queries,
    keyvals,
    attended,
    gate,
    send_sem,
    recv_sem,
    core_sem,
    pair_send,
    pair_recv,
    local_sem,
):
    side = lax.axis_index("grp")
    blk = lax.axis_index("blk")
    core = lax.axis_index("seq")
    plane, across = blk // 2, blk % 2
    mate = 1 - core
    width = HEADS * HS
    rows = image_qkv.shape[0]
    texts = text_kv.shape[0]
    own_text, own_image = 2 * texts, 2 * texts + rows

    def target(way):
        if way == UP:
            return (side, blk + 2, core)
        if way == DOWN:
            return (side, blk - 2, core)
        if way == ACROSS:
            return (side, plane * 2 + (1 - across), core)
        if way == SIDE:
            return (1 - side, blk, core)
        return (side, blk, mate)

    locals_ = [pltpu.make_async_copy(shard, weights.at[blk, core], local_sem.at[0])]
    for part, (image, text) in enumerate(((image_qkv, text_kv), (image_tan, text_tan))):
        locals_.append(
            pltpu.make_async_copy(
                image.at[:, pl.ds(0, width)], queries.at[part], local_sem.at[1 + 3 * part]
            )
        )
        locals_.append(
            pltpu.make_async_copy(
                text, keyvals.at[part, pl.ds(0, texts)], local_sem.at[2 + 3 * part]
            )
        )
        locals_.append(
            pltpu.make_async_copy(
                image.at[:, pl.ds(width, 2 * width)],
                keyvals.at[part, pl.ds(own_text, rows)],
                local_sem.at[3 + 3 * part],
            )
        )
    locals_.append(pltpu.make_async_copy(gate_table, gate, local_sem.at[7]))
    for copy in locals_:
        copy.start()

    barrier = pltpu.get_barrier_semaphore()
    for way in (ACROSS, SIDE, CORE):
        pl.semaphore_signal(barrier, inc=1, device_id=target(way), device_id_type=MESH)

    @pl.when(plane < DEPTH - 1)
    def _():
        pl.semaphore_signal(barrier, inc=1, device_id=target(UP), device_id_type=MESH)

    @pl.when(plane > 0)
    def _():
        pl.semaphore_signal(barrier, inc=1, device_id=target(DOWN), device_id_type=MESH)

    ends = (plane == 0).astype(jnp.int32) + (plane == DEPTH - 1).astype(jnp.int32)
    pl.semaphore_wait(barrier, 5 - ends)
    locals_[0].wait()

    def send(block, piece, way):
        place = weights.at[block, core, piece]
        arrived = core_sem if way == CORE else recv_sem
        return pltpu.make_async_remote_copy(
            src_ref=place,
            dst_ref=place,
            send_sem=send_sem.at[block, piece, way],
            recv_sem=arrived.at[block, piece],
            device_id=target(way),
            device_id_type=MESH,
        )

    def arrival(block, piece):
        send(block, piece, ACROSS).wait_recv()

    def mate_arrival(block, piece):
        place = weights.at[block, mate, piece]
        pltpu.make_async_remote_copy(
            src_ref=place,
            dst_ref=place,
            send_sem=send_sem.at[block, piece, CORE],
            recv_sem=core_sem.at[block, piece],
            device_id=target(CORE),
            device_id_type=MESH,
        ).wait_recv()

    def quarter(k):
        return (k + 2 * side) % QUARTERS

    other = plane * 2 + (1 - across)

    def block_at(at, flip):
        return at * 2 + (across + flip) % 2

    def both_lines(block, piece, act):
        @pl.when(plane < DEPTH - 1)
        def _():
            act(send(block, piece, UP))

        @pl.when(plane > 0)
        def _():
            act(send(block, piece, DOWN))

    def own_sends(act):
        for k in range(QUARTERS):
            piece = quarter(k)
            if k < 2:
                both_lines(blk, piece, act)
            act(send(blk, piece, ACROSS))

    def own_to_mate(act):
        for k in range(QUARTERS):
            act(send(blk, quarter(k), CORE))

    def stage(j, wait, act):
        @pl.when(j < QUARTERS)
        def _():
            piece = quarter(j)
            wait(other, piece)

            @pl.when(j == 0)
            def _():
                both_lines(other, piece, act)

            act(send(other, piece, CORE))

        @pl.when(j < 3 * (DEPTH - 1))
        def _():
            step, item = j // 3 + 1, j % 3
            flip, piece = item // 2, quarter(item % 2)
            for way, at in ((UP, plane - step), (DOWN, plane + step)):

                @pl.when((at >= 0) & (at < DEPTH))
                def _():
                    block = block_at(at, flip)
                    wait(block, piece)
                    more = plane < DEPTH - 1 if way == UP else plane > 0

                    @pl.when(more)
                    def _():
                        act(send(block, piece, way))

                    act(send(block, piece, SIDE))

                    @pl.when(item == 1)
                    def _():
                        act(send(block, piece, ACROSS))

                    act(send(block, piece, CORE))

        late = j - 2

        @pl.when((late >= 0) & (late < 3 * (DEPTH - 1)))
        def _():
            step, item = (j + 1) // 3, (j + 1) % 3
            flip, piece = item // 2, quarter(item % 2 + 2)
            for at in (plane - step, plane + step):

                @pl.when((at >= 0) & (at < DEPTH))
                def _():
                    block = block_at(at, flip)
                    wait(block, piece)

                    @pl.when(item == 1)
                    def _():
                        act(send(block, piece, ACROSS))

                    act(send(block, piece, CORE))

        @pl.when((j >= 4) & (j < 4 + 3 * (DEPTH - 1)) & ((j + 2) % 3 == 1))
        def _():
            step = (j + 2) // 3 - 1
            for at in (plane - step, plane + step):

                @pl.when((at >= 0) & (at < DEPTH))
                def _():
                    block = block_at(at, 1)
                    for k in (1, 3):
                        piece = quarter(k)
                        wait(block, piece)
                        act(send(block, piece, CORE))

    pair = []
    for part, (image, text) in enumerate(((image_qkv, text_kv), (image_tan, text_tan))):
        for nth, (source, place) in enumerate(
            (
                (text, keyvals.at[part, pl.ds(texts, texts)]),
                (image.at[:, pl.ds(width, 2 * width)], keyvals.at[part, pl.ds(own_image, rows)]),
            )
        ):
            pair.append(
                pltpu.make_async_remote_copy(
                    src_ref=source,
                    dst_ref=place,
                    send_sem=pair_send.at[2 * part + nth],
                    recv_sem=pair_recv.at[2 * part + nth],
                    device_id=target(CORE),
                    device_id_type=MESH,
                )
            )
    own_sends(lambda copy: copy.start())
    for copy in pair:
        copy.start()
    own_to_mate(lambda copy: copy.start())

    image_live, text_live = image_lengths[0], text_lengths[0]
    level = timesteps[0]
    count = 2 * (texts + rows)
    slot = lax.broadcasted_iota(jnp.int32, (1, count), 1)
    text_at = slot + jnp.where(slot < texts, core * texts, mate * texts - texts)
    image_at = slot - own_text + jnp.where(slot < own_image, core * rows, mate * rows - rows)
    position = jnp.where(slot < own_text, text_at, image_at)
    room = jnp.where(slot < own_text, text_live, image_live) - position

    def one_head(head):
        factor = HS ** (-0.5)
        lanes = pl.ds(pl.multiple_of(head * HS, HS), HS)
        value_lanes = pl.ds(pl.multiple_of(width + head * HS, HS), HS)
        q, dq = queries[0, :, lanes], queries[1, :, lanes]
        k, dk = keyvals[0, :, lanes], keyvals[1, :, lanes]
        v, dv = keyvals[0, :, value_lanes], keyvals[1, :, value_lanes]
        nt = (((1,), (1,)), ((), ()))
        scores = lax.dot_general(q, k, nt, preferred_element_type=jnp.float32) * factor
        tangent = (
            lax.dot_general(
                jnp.concatenate([dq, q], axis=1),
                jnp.concatenate([k, dk], axis=1),
                nt,
                preferred_element_type=jnp.float32,
            )
            * factor
        )
        usable = jnp.broadcast_to(room, scores.shape) > 0
        masked = jnp.where(usable, scores, -1e30)
        highest = jnp.max(masked, axis=-1, keepdims=True)
        raised = jnp.where(usable, jnp.exp(masked - highest), 0.0)
        weight = raised * (1.0 / jnp.sum(raised, axis=-1, keepdims=True))
        probs = weight.astype(jnp.bfloat16)
        product = weight * tangent
        mean = jnp.sum(product, axis=-1, keepdims=True)
        tangent_probs = (product - weight * mean).astype(jnp.bfloat16)
        both = jnp.dot(
            probs, jnp.concatenate([v, dv], axis=1), preferred_element_type=jnp.float32
        )
        moved = jnp.dot(tangent_probs, v, preferred_element_type=jnp.float32)
        attended[pl.ds(0, rows), lanes] = both[:, :HS].astype(jnp.bfloat16)
        attended[pl.ds(rows, rows), lanes] = (moved + both[:, HS:]).astype(jnp.bfloat16)

    def project(block):
        for k in range(QUARTERS):
            mate_arrival(block, k)
        share = weights[block]
        size = 2 * shard.shape[0] * shard.shape[1]
        columns = pl.ds(pl.multiple_of(block * size, 128), size)
        made = lax.dot_general(
            attended[...],
            share.reshape(size, width),
            (((1,), (1,)), ((), ())),
            preferred_element_type=jnp.float32,
        )
        made = (made * gate[pl.ds(level, 1), columns]).astype(jnp.bfloat16)
        out[:, columns] = made[:rows]
        out_tan[:, columns] = made[rows:]

    def drain(j, carry):
        stage(j, lambda block, piece: None, lambda copy: copy.wait_send())
        return carry

    def loop(j, carry):
        stage(j, arrival, lambda copy: copy.start())

        @pl.when(j == 0)
        def _():
            for copy in locals_[1:]:
                copy.wait()
            for copy in pair:
                copy.wait()

        @pl.when(j < HEADS // 2)
        def _():
            one_head(2 * j)
            one_head(2 * j + 1)

        @pl.when(j >= HEADS // 2)
        def _():
            nth = j - HEADS // 2
            at = plane + (1 - 2 * (nth % 2)) * ((nth + 1) // 2)

            @pl.when((at >= 0) & (at < DEPTH))
            def _():
                def one(flip, carry):
                    project(block_at(at, flip))
                    return carry

                lax.fori_loop(0, 2, one, 0)

        @pl.when(j >= LAG)
        def _():
            drain(j - LAG, 0)

        return carry

    lax.fori_loop(0, LAST, loop, 0)

    own_sends(lambda copy: copy.wait_send())
    own_to_mate(lambda copy: copy.wait_send())

    lax.fori_loop(LAST - LAG, LAST, drain, 0)


def fused_body(
    image_qkv,
    image_qkv_tangent,
    text_kv,
    text_kv_tangent,
    out_weight,
    gate_table,
    timesteps,
    image_lengths,
    text_lengths,
):
    rows, texts = image_qkv.shape[0], text_kv.shape[0]
    width, share = out_weight.shape
    blocks = lax.axis_size("blk")
    features = gate_table.shape[1]
    shard = out_weight.T.reshape(QUARTERS, share // QUARTERS, width)
    whole = pl.BlockSpec(memory_space=pl.ANY)
    vmem = pl.BlockSpec(memory_space=pltpu.VMEM)
    made = jax.ShapeDtypeStruct((rows, features), jnp.bfloat16)
    return tuple(
        pl.pallas_call(
            fused_kernel,
            out_shape=(made, made),
            in_specs=[pl.BlockSpec(memory_space=pltpu.SMEM)] * 3 + [whole] * 6,
            out_specs=(vmem, vmem),
            scratch_shapes=[
                pltpu.VMEM((blocks, 2, QUARTERS, share // QUARTERS, width), jnp.bfloat16),
                pltpu.VMEM((2, rows, width), jnp.bfloat16),
                pltpu.VMEM((2, 2 * (rows + texts), 2 * width), jnp.bfloat16),
                pltpu.VMEM((2 * rows, width), jnp.bfloat16),
                pltpu.VMEM(gate_table.shape, jnp.float32),
                pltpu.SemaphoreType.DMA((blocks, QUARTERS, 5)),
                pltpu.SemaphoreType.DMA((blocks, QUARTERS)),
                pltpu.SemaphoreType.DMA((blocks, QUARTERS)),
                pltpu.SemaphoreType.DMA((4,)),
                pltpu.SemaphoreType.DMA((4,)),
                pltpu.SemaphoreType.DMA((8,)),
            ],
            compiler_params=pltpu.CompilerParams(
                collective_id=0, has_side_effects=True, vmem_limit_bytes=60 * 1024 * 1024
            ),
        )(
            timesteps,
            image_lengths,
            text_lengths,
            shard,
            image_qkv,
            image_qkv_tangent,
            text_kv,
            text_kv_tangent,
            gate_table,
        )
    )


def fits(mesh):
    sizes = dict(mesh.shape)
    return sizes["grp"] == 2 and sizes["seq"] == 2 and sizes["blk"] == 2 * DEPTH


def solution(mesh):
    in_specs = (
        P(("grp", "blk", "seq"), None),
        P(("grp", "blk", "seq"), None),
        P(("grp", "blk", "seq"), None),
        P(("grp", "blk", "seq"), None),
        P(None, ("blk", "seq")),
        P(),
        P(("grp", "blk")),
        P(("grp", "blk")),
        P(("grp", "blk")),
    )
    out_specs = (P(("grp", "blk", "seq"), None), P(("grp", "blk", "seq"), None))
    chosen = fused_body if fits(mesh) else body
    return jax.shard_map(chosen, mesh=mesh, in_specs=in_specs, out_specs=out_specs, check_vma=False)
```

```python
import jax
import jax.numpy as jnp
from jax import lax
from jax.experimental import pallas as pl
from jax.experimental.pallas import tpu as pltpu
from jax.sharding import PartitionSpec as P

HS = 128
HEADS = 12


def attend(queries, tangent_queries, all_keys, tangent_keys, all_values, tangent_values, usable):
    factor = HS ** (-0.5)
    scores = (
        jnp.einsum("qhd,khd->hqk", queries, all_keys, preferred_element_type=jnp.float32) * factor
    )
    tangent_scores = (
        jnp.einsum("qhd,khd->hqk", tangent_queries, all_keys, preferred_element_type=jnp.float32)
        + jnp.einsum("qhd,khd->hqk", queries, tangent_keys, preferred_element_type=jnp.float32)
    ) * factor
    masked = jnp.where(usable[None, None, :], scores, -1e30)
    highest = jnp.max(masked, axis=-1, keepdims=True)
    raised = jnp.where(usable[None, None, :], jnp.exp(masked - highest), 0.0)
    weights = raised / jnp.sum(raised, axis=-1, keepdims=True)
    probs = weights.astype(jnp.bfloat16)
    centred = tangent_scores - jnp.sum(weights * tangent_scores, axis=-1, keepdims=True)
    tangent_probs = (weights * centred).astype(jnp.bfloat16)
    attended = jnp.einsum("hqk,khd->qhd", probs, all_values, preferred_element_type=jnp.float32)
    tangent_attended = jnp.einsum(
        "hqk,khd->qhd", tangent_probs, all_values, preferred_element_type=jnp.float32
    ) + jnp.einsum("hqk,khd->qhd", probs, tangent_values, preferred_element_type=jnp.float32)
    return (attended.astype(jnp.bfloat16), tangent_attended.astype(jnp.bfloat16))


def column_projector(stacked_rows, shard_piece):
    return jnp.dot(stacked_rows, shard_piece, preferred_element_type=jnp.float32)


def body(
    image_qkv,
    image_qkv_tangent,
    text_kv,
    text_kv_tangent,
    out_weight,
    gate_table,
    timesteps,
    image_lengths,
    text_lengths,
):
    row_count = image_qkv.shape[0]
    text_count = text_kv.shape[0]
    seq_count = lax.axis_size("seq")
    local_heads = HEADS // seq_count
    image_primal = image_qkv.reshape(row_count, 3, seq_count, local_heads, HS)
    image_tangent = image_qkv_tangent.reshape(row_count, 3, seq_count, local_heads, HS)
    text_primal = text_kv.reshape(text_count, 2, seq_count, local_heads, HS)
    text_tangent = text_kv_tangent.reshape(text_count, 2, seq_count, local_heads, HS)
    image_live = image_lengths[0]
    text_live = text_lengths[0]
    primal = lax.all_to_all(image_primal, "seq", split_axis=2, concat_axis=0, tiled=True)[:, :, 0]
    tangent = lax.all_to_all(image_tangent, "seq", split_axis=2, concat_axis=0, tiled=True)[:, :, 0]
    text_part = lax.all_to_all(text_primal, "seq", split_axis=2, concat_axis=0, tiled=True)[:, :, 0]
    text_tan = lax.all_to_all(text_tangent, "seq", split_axis=2, concat_axis=0, tiled=True)[:, :, 0]
    usable = jnp.concatenate(
        [
            jnp.arange(text_part.shape[0], dtype=jnp.int32) < text_live,
            jnp.arange(primal.shape[0], dtype=jnp.int32) < image_live,
        ],
        axis=0,
    )
    all_keys = jnp.concatenate([text_part[:, 0], primal[:, 1]], axis=0)
    tangent_keys = jnp.concatenate([text_tan[:, 0], tangent[:, 1]], axis=0)
    all_values = jnp.concatenate([text_part[:, 1], primal[:, 2]], axis=0)
    tangent_values = jnp.concatenate([text_tan[:, 1], tangent[:, 2]], axis=0)
    attended, tangent_attended = attend(
        primal[:, 0], tangent[:, 0], all_keys, tangent_keys, all_values, tangent_values, usable
    )
    gate_row = lax.dynamic_index_in_dim(gate_table, timesteps[0], 0, keepdims=False)
    local_primal, local_tangent = (
        lax.all_to_all(attended, "seq", split_axis=0, concat_axis=1, tiled=True),
        lax.all_to_all(tangent_attended, "seq", split_axis=0, concat_axis=1, tiled=True),
    )
    stacked_rows = jnp.concatenate(
        [local_primal.reshape(row_count, HEADS * HS), local_tangent.reshape(row_count, HEADS * HS)],
        axis=0,
    )
    projected = column_projector(
        stacked_rows, lax.all_gather(out_weight, ("blk", "seq"), axis=1, tiled=True)
    )
    output = (projected[:row_count] * gate_row).astype(jnp.bfloat16)
    output_tangent = (projected[row_count:] * gate_row).astype(jnp.bfloat16)
    return (output, output_tangent)


MESH = pl.DeviceIdType.MESH
DEPTH = 4
QUARTERS = 4
LAST = 13
LAG = 4
UP, DOWN, ACROSS, SIDE, CORE = 0, 1, 2, 3, 4


def fused_kernel(
    timesteps,
    image_lengths,
    text_lengths,
    shard,
    image_qkv,
    image_tan,
    text_kv,
    text_tan,
    gate_table,
    out,
    out_tan,
    weights,
    queries,
    keyvals,
    attended,
    gate,
    held,
    out_sem,
    send_sem,
    recv_sem,
    core_sem,
    pair_send,
    pair_recv,
    local_sem,
):
    side = lax.axis_index("grp")
    blk = lax.axis_index("blk")
    core = lax.axis_index("seq")
    plane, across = blk // 2, blk % 2
    mate = 1 - core
    width = HEADS * HS
    rows = image_qkv.shape[0]
    texts = text_kv.shape[0]
    own_text, own_image = 2 * texts, 2 * texts + rows

    def target(way):
        if way == UP:
            return (side, blk + 2, core)
        if way == DOWN:
            return (side, blk - 2, core)
        if way == ACROSS:
            return (side, plane * 2 + (1 - across), core)
        if way == SIDE:
            return (1 - side, blk, core)
        return (side, blk, mate)

    locals_ = [pltpu.make_async_copy(shard, weights.at[blk, core], local_sem.at[0])]
    for part, (image, text) in enumerate(((image_qkv, text_kv), (image_tan, text_tan))):
        locals_.append(
            pltpu.make_async_copy(
                image.at[:, pl.ds(0, width)], queries.at[part], local_sem.at[1 + 3 * part]
            )
        )
        locals_.append(
            pltpu.make_async_copy(
                text, keyvals.at[part, pl.ds(0, texts)], local_sem.at[2 + 3 * part]
            )
        )
        locals_.append(
            pltpu.make_async_copy(
                image.at[:, pl.ds(width, 2 * width)],
                keyvals.at[part, pl.ds(own_text, rows)],
                local_sem.at[3 + 3 * part],
            )
        )
    locals_.append(pltpu.make_async_copy(gate_table, gate, local_sem.at[7]))
    for copy in locals_:
        copy.start()

    barrier = pltpu.get_barrier_semaphore()
    for way in (ACROSS, SIDE, CORE):
        pl.semaphore_signal(barrier, inc=1, device_id=target(way), device_id_type=MESH)

    @pl.when(plane < DEPTH - 1)
    def _():
        pl.semaphore_signal(barrier, inc=1, device_id=target(UP), device_id_type=MESH)

    @pl.when(plane > 0)
    def _():
        pl.semaphore_signal(barrier, inc=1, device_id=target(DOWN), device_id_type=MESH)

    ends = (plane == 0).astype(jnp.int32) + (plane == DEPTH - 1).astype(jnp.int32)
    pl.semaphore_wait(barrier, 5 - ends)
    locals_[0].wait()

    def send(block, piece, way):
        place = weights.at[block, core, piece]
        arrived = core_sem if way == CORE else recv_sem
        return pltpu.make_async_remote_copy(
            src_ref=place,
            dst_ref=place,
            send_sem=send_sem.at[block, piece, way],
            recv_sem=arrived.at[block, piece],
            device_id=target(way),
            device_id_type=MESH,
        )

    def arrival(block, piece):
        send(block, piece, ACROSS).wait_recv()

    def mate_arrival(block, piece):
        place = weights.at[block, mate, piece]
        pltpu.make_async_remote_copy(
            src_ref=place,
            dst_ref=place,
            send_sem=send_sem.at[block, piece, CORE],
            recv_sem=core_sem.at[block, piece],
            device_id=target(CORE),
            device_id_type=MESH,
        ).wait_recv()

    def quarter(k):
        return (k + 2 * side) % QUARTERS

    other = plane * 2 + (1 - across)

    def block_at(at, flip):
        return at * 2 + (across + flip) % 2

    def both_lines(block, piece, act):
        @pl.when(plane < DEPTH - 1)
        def _():
            act(send(block, piece, UP))

        @pl.when(plane > 0)
        def _():
            act(send(block, piece, DOWN))

    def own_sends(act):
        for k in range(QUARTERS):
            piece = quarter(k)
            if k < 2:
                both_lines(blk, piece, act)
            act(send(blk, piece, ACROSS))

    def own_to_mate(act):
        for k in range(QUARTERS):
            act(send(blk, quarter(k), CORE))

    def stage(j, wait, act):
        @pl.when(j < QUARTERS)
        def _():
            piece = quarter(j)
            wait(other, piece)

            @pl.when(j == 0)
            def _():
                both_lines(other, piece, act)

            act(send(other, piece, CORE))

        @pl.when(j < 3 * (DEPTH - 1))
        def _():
            step, item = j // 3 + 1, j % 3
            flip, piece = item // 2, quarter(item % 2)
            for way, at in ((UP, plane - step), (DOWN, plane + step)):

                @pl.when((at >= 0) & (at < DEPTH))
                def _():
                    block = block_at(at, flip)
                    wait(block, piece)
                    more = plane < DEPTH - 1 if way == UP else plane > 0

                    @pl.when(more)
                    def _():
                        act(send(block, piece, way))

                    act(send(block, piece, SIDE))

                    @pl.when(item == 1)
                    def _():
                        act(send(block, piece, ACROSS))

                    act(send(block, piece, CORE))

        late = j - 2

        @pl.when((late >= 0) & (late < 3 * (DEPTH - 1)))
        def _():
            step, item = (j + 1) // 3, (j + 1) % 3
            flip, piece = item // 2, quarter(item % 2 + 2)
            for at in (plane - step, plane + step):

                @pl.when((at >= 0) & (at < DEPTH))
                def _():
                    block = block_at(at, flip)
                    wait(block, piece)

                    @pl.when(item == 1)
                    def _():
                        act(send(block, piece, ACROSS))

                    act(send(block, piece, CORE))

        @pl.when((j >= 4) & (j < 4 + 3 * (DEPTH - 1)) & ((j + 2) % 3 == 1))
        def _():
            step = (j + 2) // 3 - 1
            for at in (plane - step, plane + step):

                @pl.when((at >= 0) & (at < DEPTH))
                def _():
                    block = block_at(at, 1)
                    for k in (1, 3):
                        piece = quarter(k)
                        wait(block, piece)
                        act(send(block, piece, CORE))

    pair = []
    for part, (image, text) in enumerate(((image_qkv, text_kv), (image_tan, text_tan))):
        for nth, (source, place) in enumerate(
            (
                (text, keyvals.at[part, pl.ds(texts, texts)]),
                (image.at[:, pl.ds(width, 2 * width)], keyvals.at[part, pl.ds(own_image, rows)]),
            )
        ):
            pair.append(
                pltpu.make_async_remote_copy(
                    src_ref=source,
                    dst_ref=place,
                    send_sem=pair_send.at[2 * part + nth],
                    recv_sem=pair_recv.at[2 * part + nth],
                    device_id=target(CORE),
                    device_id_type=MESH,
                )
            )
    own_sends(lambda copy: copy.start())
    for copy in pair:
        copy.start()
    own_to_mate(lambda copy: copy.start())

    image_live, text_live = image_lengths[0], text_lengths[0]
    level = timesteps[0]
    count = 2 * (texts + rows)
    slot = lax.broadcasted_iota(jnp.int32, (1, count), 1)
    text_at = slot + jnp.where(slot < texts, core * texts, mate * texts - texts)
    image_at = slot - own_text + jnp.where(slot < own_image, core * rows, mate * rows - rows)
    position = jnp.where(slot < own_text, text_at, image_at)
    room = jnp.where(slot < own_text, text_live, image_live) - position

    def one_head(head):
        factor = HS ** (-0.5)
        lanes = pl.ds(pl.multiple_of(head * HS, HS), HS)
        value_lanes = pl.ds(pl.multiple_of(width + head * HS, HS), HS)
        q, dq = queries[0, :, lanes], queries[1, :, lanes]
        k, dk = keyvals[0, :, lanes], keyvals[1, :, lanes]
        v, dv = keyvals[0, :, value_lanes], keyvals[1, :, value_lanes]
        nt = (((1,), (1,)), ((), ()))
        scores = lax.dot_general(q, k, nt, preferred_element_type=jnp.float32) * factor
        tangent = (
            lax.dot_general(
                jnp.concatenate([dq, q], axis=1),
                jnp.concatenate([k, dk], axis=1),
                nt,
                preferred_element_type=jnp.float32,
            )
            * factor
        )
        usable = jnp.broadcast_to(room, scores.shape) > 0
        masked = jnp.where(usable, scores, -1e30)
        highest = jnp.max(masked, axis=-1, keepdims=True)
        raised = jnp.where(usable, jnp.exp(masked - highest), 0.0)
        weight = raised * (1.0 / jnp.sum(raised, axis=-1, keepdims=True))
        probs = weight.astype(jnp.bfloat16)
        product = weight * tangent
        mean = jnp.sum(product, axis=-1, keepdims=True)
        tangent_probs = (product - weight * mean).astype(jnp.bfloat16)
        both = jnp.dot(
            probs, jnp.concatenate([v, dv], axis=1), preferred_element_type=jnp.float32
        )
        moved = jnp.dot(tangent_probs, v, preferred_element_type=jnp.float32)
        attended[pl.ds(0, rows), lanes] = both[:, :HS].astype(jnp.bfloat16)
        attended[pl.ds(rows, rows), lanes] = (moved + both[:, HS:]).astype(jnp.bfloat16)

    def leave(block):
        size = 2 * shard.shape[0] * shard.shape[1]
        columns = pl.ds(pl.multiple_of(block * size, 128), size)
        return [
            pltpu.make_async_copy(
                held.at[pl.ds(part * rows, rows), columns],
                place.at[:, columns],
                out_sem.at[block, part],
            )
            for part, place in enumerate((out, out_tan))
        ]

    def project(block):
        for k in range(QUARTERS):
            mate_arrival(block, k)
        share = weights[block]
        size = 2 * shard.shape[0] * shard.shape[1]
        columns = pl.ds(pl.multiple_of(block * size, 128), size)
        made = lax.dot_general(
            attended[...],
            share.reshape(size, width),
            (((1,), (1,)), ((), ())),
            preferred_element_type=jnp.float32,
        )
        made = (made * gate[pl.ds(level, 1), columns]).astype(jnp.bfloat16)
        held[:, columns] = made
        for copy in leave(block):
            copy.start()

    def drain(j, carry):
        stage(j, lambda block, piece: None, lambda copy: copy.wait_send())
        return carry

    def loop(j, carry):
        stage(j, arrival, lambda copy: copy.start())

        @pl.when(j == 0)
        def _():
            for copy in locals_[1:]:
                copy.wait()
            for copy in pair:
                copy.wait()

        @pl.when(j < HEADS // 2)
        def _():
            one_head(2 * j)
            one_head(2 * j + 1)

        @pl.when(j >= HEADS // 2)
        def _():
            nth = j - HEADS // 2
            at = plane + (1 - 2 * (nth % 2)) * ((nth + 1) // 2)

            @pl.when((at >= 0) & (at < DEPTH))
            def _():
                def one(flip, carry):
                    project(block_at(at, flip))
                    return carry

                lax.fori_loop(0, 2, one, 0)

        @pl.when(j >= LAG)
        def _():
            drain(j - LAG, 0)

        return carry

    lax.fori_loop(0, LAST, loop, 0)

    own_sends(lambda copy: copy.wait_send())
    own_to_mate(lambda copy: copy.wait_send())

    lax.fori_loop(LAST - LAG, LAST, drain, 0)

    def left(block, carry):
        for copy in leave(block):
            copy.wait()
        return carry

    lax.fori_loop(0, 2 * DEPTH, left, 0)


def fused_body(
    image_qkv,
    image_qkv_tangent,
    text_kv,
    text_kv_tangent,
    out_weight,
    gate_table,
    timesteps,
    image_lengths,
    text_lengths,
):
    rows, texts = image_qkv.shape[0], text_kv.shape[0]
    width, share = out_weight.shape
    blocks = lax.axis_size("blk")
    features = gate_table.shape[1]
    shard = out_weight.T.reshape(QUARTERS, share // QUARTERS, width)
    whole = pl.BlockSpec(memory_space=pl.ANY)
    vmem = pl.BlockSpec(memory_space=pltpu.VMEM)
    made = jax.ShapeDtypeStruct((rows, features), jnp.bfloat16)
    return tuple(
        pl.pallas_call(
            fused_kernel,
            out_shape=(made, made),
            in_specs=[pl.BlockSpec(memory_space=pltpu.SMEM)] * 3 + [whole] * 6,
            out_specs=(whole, whole),
            scratch_shapes=[
                pltpu.VMEM((blocks, 2, QUARTERS, share // QUARTERS, width), jnp.bfloat16),
                pltpu.VMEM((2, rows, width), jnp.bfloat16),
                pltpu.VMEM((2, 2 * (rows + texts), 2 * width), jnp.bfloat16),
                pltpu.VMEM((2 * rows, width), jnp.bfloat16),
                pltpu.VMEM(gate_table.shape, jnp.float32),
                pltpu.VMEM((2 * rows, features), jnp.bfloat16),
                pltpu.SemaphoreType.DMA((blocks, 2)),
                pltpu.SemaphoreType.DMA((blocks, QUARTERS, 5)),
                pltpu.SemaphoreType.DMA((blocks, QUARTERS)),
                pltpu.SemaphoreType.DMA((blocks, QUARTERS)),
                pltpu.SemaphoreType.DMA((4,)),
                pltpu.SemaphoreType.DMA((4,)),
                pltpu.SemaphoreType.DMA((8,)),
            ],
            compiler_params=pltpu.CompilerParams(
                collective_id=0, has_side_effects=True, vmem_limit_bytes=62 * 1024 * 1024
            ),
        )(
            timesteps,
            image_lengths,
            text_lengths,
            shard,
            image_qkv,
            image_qkv_tangent,
            text_kv,
            text_kv_tangent,
            gate_table,
        )
    )


def fits(mesh):
    sizes = dict(mesh.shape)
    return sizes["grp"] == 2 and sizes["seq"] == 2 and sizes["blk"] == 2 * DEPTH


def solution(mesh):
    in_specs = (
        P(("grp", "blk", "seq"), None),
        P(("grp", "blk", "seq"), None),
        P(("grp", "blk", "seq"), None),
        P(("grp", "blk", "seq"), None),
        P(None, ("blk", "seq")),
        P(),
        P(("grp", "blk")),
        P(("grp", "blk")),
        P(("grp", "blk")),
    )
    out_specs = (P(("grp", "blk", "seq"), None), P(("grp", "blk", "seq"), None))
    chosen = fused_body if fits(mesh) else body
    return jax.shard_map(chosen, mesh=mesh, in_specs=in_specs, out_specs=out_specs, check_vma=False)
```

```python
import jax
import jax.numpy as jnp
from jax import lax
from jax.experimental import pallas as pl
from jax.experimental.pallas import tpu as pltpu
from jax.sharding import PartitionSpec as P

HS = 128
HEADS = 12


def attend(queries, tangent_queries, all_keys, tangent_keys, all_values, tangent_values, usable):
    factor = HS ** (-0.5)
    scores = (
        jnp.einsum("qhd,khd->hqk", queries, all_keys, preferred_element_type=jnp.float32) * factor
    )
    tangent_scores = (
        jnp.einsum("qhd,khd->hqk", tangent_queries, all_keys, preferred_element_type=jnp.float32)
        + jnp.einsum("qhd,khd->hqk", queries, tangent_keys, preferred_element_type=jnp.float32)
    ) * factor
    masked = jnp.where(usable[None, None, :], scores, -1e30)
    highest = jnp.max(masked, axis=-1, keepdims=True)
    raised = jnp.where(usable[None, None, :], jnp.exp(masked - highest), 0.0)
    weights = raised / jnp.sum(raised, axis=-1, keepdims=True)
    probs = weights.astype(jnp.bfloat16)
    centred = tangent_scores - jnp.sum(weights * tangent_scores, axis=-1, keepdims=True)
    tangent_probs = (weights * centred).astype(jnp.bfloat16)
    attended = jnp.einsum("hqk,khd->qhd", probs, all_values, preferred_element_type=jnp.float32)
    tangent_attended = jnp.einsum(
        "hqk,khd->qhd", tangent_probs, all_values, preferred_element_type=jnp.float32
    ) + jnp.einsum("hqk,khd->qhd", probs, tangent_values, preferred_element_type=jnp.float32)
    return (attended.astype(jnp.bfloat16), tangent_attended.astype(jnp.bfloat16))


def column_projector(stacked_rows, shard_piece):
    return jnp.dot(stacked_rows, shard_piece, preferred_element_type=jnp.float32)


def body(
    image_qkv,
    image_qkv_tangent,
    text_kv,
    text_kv_tangent,
    out_weight,
    gate_table,
    timesteps,
    image_lengths,
    text_lengths,
):
    row_count = image_qkv.shape[0]
    text_count = text_kv.shape[0]
    seq_count = lax.axis_size("seq")
    local_heads = HEADS // seq_count
    image_primal = image_qkv.reshape(row_count, 3, seq_count, local_heads, HS)
    image_tangent = image_qkv_tangent.reshape(row_count, 3, seq_count, local_heads, HS)
    text_primal = text_kv.reshape(text_count, 2, seq_count, local_heads, HS)
    text_tangent = text_kv_tangent.reshape(text_count, 2, seq_count, local_heads, HS)
    image_live = image_lengths[0]
    text_live = text_lengths[0]
    primal = lax.all_to_all(image_primal, "seq", split_axis=2, concat_axis=0, tiled=True)[:, :, 0]
    tangent = lax.all_to_all(image_tangent, "seq", split_axis=2, concat_axis=0, tiled=True)[:, :, 0]
    text_part = lax.all_to_all(text_primal, "seq", split_axis=2, concat_axis=0, tiled=True)[:, :, 0]
    text_tan = lax.all_to_all(text_tangent, "seq", split_axis=2, concat_axis=0, tiled=True)[:, :, 0]
    usable = jnp.concatenate(
        [
            jnp.arange(text_part.shape[0], dtype=jnp.int32) < text_live,
            jnp.arange(primal.shape[0], dtype=jnp.int32) < image_live,
        ],
        axis=0,
    )
    all_keys = jnp.concatenate([text_part[:, 0], primal[:, 1]], axis=0)
    tangent_keys = jnp.concatenate([text_tan[:, 0], tangent[:, 1]], axis=0)
    all_values = jnp.concatenate([text_part[:, 1], primal[:, 2]], axis=0)
    tangent_values = jnp.concatenate([text_tan[:, 1], tangent[:, 2]], axis=0)
    attended, tangent_attended = attend(
        primal[:, 0], tangent[:, 0], all_keys, tangent_keys, all_values, tangent_values, usable
    )
    gate_row = lax.dynamic_index_in_dim(gate_table, timesteps[0], 0, keepdims=False)
    local_primal, local_tangent = (
        lax.all_to_all(attended, "seq", split_axis=0, concat_axis=1, tiled=True),
        lax.all_to_all(tangent_attended, "seq", split_axis=0, concat_axis=1, tiled=True),
    )
    stacked_rows = jnp.concatenate(
        [local_primal.reshape(row_count, HEADS * HS), local_tangent.reshape(row_count, HEADS * HS)],
        axis=0,
    )
    projected = column_projector(
        stacked_rows, lax.all_gather(out_weight, ("blk", "seq"), axis=1, tiled=True)
    )
    output = (projected[:row_count] * gate_row).astype(jnp.bfloat16)
    output_tangent = (projected[row_count:] * gate_row).astype(jnp.bfloat16)
    return (output, output_tangent)


MESH = pl.DeviceIdType.MESH
DEPTH = 4
QUARTERS = 4
LAST = 13
LAG = 4
UP, DOWN, ACROSS, SIDE, CORE = 0, 1, 2, 3, 4


def fused_kernel(
    timesteps,
    image_lengths,
    text_lengths,
    shard,
    image_qkv,
    image_tan,
    text_kv,
    text_tan,
    gate_table,
    out,
    out_tan,
    weights,
    queries,
    keyvals,
    attended,
    gate,
    held,
    out_sem,
    send_sem,
    recv_sem,
    core_sem,
    pair_send,
    pair_recv,
    local_sem,
):
    side = lax.axis_index("grp")
    blk = lax.axis_index("blk")
    core = lax.axis_index("seq")
    plane, across = blk // 2, blk % 2
    mate = 1 - core
    width = HEADS * HS
    rows = image_qkv.shape[0]
    texts = text_kv.shape[0]
    own_text, own_image = 2 * texts, 2 * texts + rows

    def target(way):
        if way == UP:
            return (side, blk + 2, core)
        if way == DOWN:
            return (side, blk - 2, core)
        if way == ACROSS:
            return (side, plane * 2 + (1 - across), core)
        if way == SIDE:
            return (1 - side, blk, core)
        return (side, blk, mate)

    locals_ = [pltpu.make_async_copy(shard, weights.at[blk, core], local_sem.at[0])]
    for part, (image, text) in enumerate(((image_qkv, text_kv), (image_tan, text_tan))):
        locals_.append(
            pltpu.make_async_copy(
                image.at[:, pl.ds(0, width)], queries.at[part], local_sem.at[1 + 3 * part]
            )
        )
        locals_.append(
            pltpu.make_async_copy(
                text, keyvals.at[part, pl.ds(0, texts)], local_sem.at[2 + 3 * part]
            )
        )
        locals_.append(
            pltpu.make_async_copy(
                image.at[:, pl.ds(width, 2 * width)],
                keyvals.at[part, pl.ds(own_text, rows)],
                local_sem.at[3 + 3 * part],
            )
        )
    locals_.append(pltpu.make_async_copy(gate_table, gate, local_sem.at[7]))
    for copy in locals_:
        copy.start()

    barrier = pltpu.get_barrier_semaphore()
    for way in (ACROSS, SIDE, CORE):
        pl.semaphore_signal(barrier, inc=1, device_id=target(way), device_id_type=MESH)

    @pl.when(plane < DEPTH - 1)
    def _():
        pl.semaphore_signal(barrier, inc=1, device_id=target(UP), device_id_type=MESH)

    @pl.when(plane > 0)
    def _():
        pl.semaphore_signal(barrier, inc=1, device_id=target(DOWN), device_id_type=MESH)

    ends = (plane == 0).astype(jnp.int32) + (plane == DEPTH - 1).astype(jnp.int32)
    pl.semaphore_wait(barrier, 5 - ends)
    locals_[0].wait()

    def send(block, piece, way):
        place = weights.at[block, core, piece]
        arrived = core_sem if way == CORE else recv_sem
        return pltpu.make_async_remote_copy(
            src_ref=place,
            dst_ref=place,
            send_sem=send_sem.at[block, piece, way],
            recv_sem=arrived.at[block, piece],
            device_id=target(way),
            device_id_type=MESH,
        )

    def arrival(block, piece):
        send(block, piece, ACROSS).wait_recv()

    def mate_arrival(block, piece):
        place = weights.at[block, mate, piece]
        pltpu.make_async_remote_copy(
            src_ref=place,
            dst_ref=place,
            send_sem=send_sem.at[block, piece, CORE],
            recv_sem=core_sem.at[block, piece],
            device_id=target(CORE),
            device_id_type=MESH,
        ).wait_recv()

    def quarter(k):
        return (k + 2 * side) % QUARTERS

    other = plane * 2 + (1 - across)

    def block_at(at, flip):
        return at * 2 + (across + flip) % 2

    def both_lines(block, piece, act):
        @pl.when(plane < DEPTH - 1)
        def _():
            act(send(block, piece, UP))

        @pl.when(plane > 0)
        def _():
            act(send(block, piece, DOWN))

    def own_sends(act):
        act(send(blk, quarter(0), ACROSS))
        for k in range(2):
            both_lines(blk, quarter(k), act)

    def own_to_mate(act):
        for k in range(QUARTERS):
            act(send(blk, quarter(k), CORE))

    def stage(j, wait, act):
        @pl.when(j < QUARTERS)
        def _():
            piece = quarter(j)
            wait(other, piece)

            @pl.when(j == 0)
            def _():
                both_lines(other, piece, act)
                for k in range(1, QUARTERS):
                    act(send(blk, quarter(k), ACROSS))

            act(send(other, piece, CORE))

        @pl.when(j < 3 * (DEPTH - 1))
        def _():
            step, item = j // 3 + 1, j % 3
            flip, piece = item // 2, quarter(item % 2)
            for way, at in ((UP, plane - step), (DOWN, plane + step)):

                @pl.when((at >= 0) & (at < DEPTH))
                def _():
                    block = block_at(at, flip)
                    wait(block, piece)
                    more = plane < DEPTH - 1 if way == UP else plane > 0

                    @pl.when(more)
                    def _():
                        act(send(block, piece, way))

                    act(send(block, piece, SIDE))

                    @pl.when(item == 1)
                    def _():
                        act(send(block, piece, ACROSS))

                    act(send(block, piece, CORE))

        late = j - 2

        @pl.when((late >= 0) & (late < 3 * (DEPTH - 1)))
        def _():
            step, item = (j + 1) // 3, (j + 1) % 3
            flip, piece = item // 2, quarter(item % 2 + 2)
            for at in (plane - step, plane + step):

                @pl.when((at >= 0) & (at < DEPTH))
                def _():
                    block = block_at(at, flip)
                    wait(block, piece)

                    @pl.when(item == 1)
                    def _():
                        act(send(block, piece, ACROSS))

                    act(send(block, piece, CORE))

        @pl.when((j >= 4) & (j < 4 + 3 * (DEPTH - 1)) & ((j + 2) % 3 == 1))
        def _():
            step = (j + 2) // 3 - 1
            for at in (plane - step, plane + step):

                @pl.when((at >= 0) & (at < DEPTH))
                def _():
                    block = block_at(at, 1)
                    for k in (1, 3):
                        piece = quarter(k)
                        wait(block, piece)
                        act(send(block, piece, CORE))

    pair = []
    for part, (image, text) in enumerate(((image_qkv, text_kv), (image_tan, text_tan))):
        for nth, (source, place) in enumerate(
            (
                (text, keyvals.at[part, pl.ds(texts, texts)]),
                (image.at[:, pl.ds(width, 2 * width)], keyvals.at[part, pl.ds(own_image, rows)]),
            )
        ):
            pair.append(
                pltpu.make_async_remote_copy(
                    src_ref=source,
                    dst_ref=place,
                    send_sem=pair_send.at[2 * part + nth],
                    recv_sem=pair_recv.at[2 * part + nth],
                    device_id=target(CORE),
                    device_id_type=MESH,
                )
            )
    own_sends(lambda copy: copy.start())
    for copy in pair:
        copy.start()
    own_to_mate(lambda copy: copy.start())

    image_live, text_live = image_lengths[0], text_lengths[0]
    level = timesteps[0]
    count = 2 * (texts + rows)
    slot = lax.broadcasted_iota(jnp.int32, (1, count), 1)
    text_at = slot + jnp.where(slot < texts, core * texts, mate * texts - texts)
    image_at = slot - own_text + jnp.where(slot < own_image, core * rows, mate * rows - rows)
    position = jnp.where(slot < own_text, text_at, image_at)
    room = jnp.where(slot < own_text, text_live, image_live) - position

    def one_head(head):
        factor = HS ** (-0.5)
        lanes = pl.ds(pl.multiple_of(head * HS, HS), HS)
        value_lanes = pl.ds(pl.multiple_of(width + head * HS, HS), HS)
        q, dq = queries[0, :, lanes], queries[1, :, lanes]
        k, dk = keyvals[0, :, lanes], keyvals[1, :, lanes]
        v, dv = keyvals[0, :, value_lanes], keyvals[1, :, value_lanes]
        nt = (((1,), (1,)), ((), ()))
        scores = lax.dot_general(q, k, nt, preferred_element_type=jnp.float32) * factor
        tangent = (
            lax.dot_general(
                jnp.concatenate([dq, q], axis=1),
                jnp.concatenate([k, dk], axis=1),
                nt,
                preferred_element_type=jnp.float32,
            )
            * factor
        )
        usable = jnp.broadcast_to(room, scores.shape) > 0
        masked = jnp.where(usable, scores, -1e30)
        highest = jnp.max(masked, axis=-1, keepdims=True)
        raised = jnp.where(usable, jnp.exp(masked - highest), 0.0)
        weight = raised * (1.0 / jnp.sum(raised, axis=-1, keepdims=True))
        probs = weight.astype(jnp.bfloat16)
        product = weight * tangent
        mean = jnp.sum(product, axis=-1, keepdims=True)
        tangent_probs = (product - weight * mean).astype(jnp.bfloat16)
        both = jnp.dot(
            probs, jnp.concatenate([v, dv], axis=1), preferred_element_type=jnp.float32
        )
        moved = jnp.dot(tangent_probs, v, preferred_element_type=jnp.float32)
        attended[pl.ds(0, rows), lanes] = both[:, :HS].astype(jnp.bfloat16)
        attended[pl.ds(rows, rows), lanes] = (moved + both[:, HS:]).astype(jnp.bfloat16)

    def leave(block):
        size = 2 * shard.shape[0] * shard.shape[1]
        columns = pl.ds(pl.multiple_of(block * size, 128), size)
        return [
            pltpu.make_async_copy(
                held.at[pl.ds(part * rows, rows), columns],
                place.at[:, columns],
                out_sem.at[block, part],
            )
            for part, place in enumerate((out, out_tan))
        ]

    def project(block):
        for k in range(QUARTERS):
            mate_arrival(block, k)
        share = weights[block]
        size = 2 * shard.shape[0] * shard.shape[1]
        columns = pl.ds(pl.multiple_of(block * size, 128), size)
        made = lax.dot_general(
            attended[...],
            share.reshape(size, width),
            (((1,), (1,)), ((), ())),
            preferred_element_type=jnp.float32,
        )
        made = (made * gate[pl.ds(level, 1), columns]).astype(jnp.bfloat16)
        held[:, columns] = made
        for copy in leave(block):
            copy.start()

    def drain(j, carry):
        stage(j, lambda block, piece: None, lambda copy: copy.wait_send())
        return carry

    def loop(j, carry):
        stage(j, arrival, lambda copy: copy.start())

        @pl.when(j == 0)
        def _():
            for copy in locals_[1:]:
                copy.wait()
            for copy in pair:
                copy.wait()

        @pl.when(j < HEADS // 2)
        def _():
            one_head(2 * j)
            one_head(2 * j + 1)

        @pl.when(j >= HEADS // 2)
        def _():
            nth = j - HEADS // 2
            at = plane + (1 - 2 * (nth % 2)) * ((nth + 1) // 2)

            @pl.when((at >= 0) & (at < DEPTH))
            def _():
                def one(flip, carry):
                    project(block_at(at, flip))
                    return carry

                lax.fori_loop(0, 2, one, 0)

        @pl.when(j >= LAG)
        def _():
            drain(j - LAG, 0)

        return carry

    lax.fori_loop(0, LAST, loop, 0)

    own_sends(lambda copy: copy.wait_send())
    own_to_mate(lambda copy: copy.wait_send())

    lax.fori_loop(LAST - LAG, LAST, drain, 0)

    def left(block, carry):
        for copy in leave(block):
            copy.wait()
        return carry

    lax.fori_loop(0, 2 * DEPTH, left, 0)


def fused_body(
    image_qkv,
    image_qkv_tangent,
    text_kv,
    text_kv_tangent,
    out_weight,
    gate_table,
    timesteps,
    image_lengths,
    text_lengths,
):
    rows, texts = image_qkv.shape[0], text_kv.shape[0]
    width, share = out_weight.shape
    blocks = lax.axis_size("blk")
    features = gate_table.shape[1]
    shard = out_weight.T.reshape(QUARTERS, share // QUARTERS, width)
    whole = pl.BlockSpec(memory_space=pl.ANY)
    vmem = pl.BlockSpec(memory_space=pltpu.VMEM)
    made = jax.ShapeDtypeStruct((rows, features), jnp.bfloat16)
    return tuple(
        pl.pallas_call(
            fused_kernel,
            out_shape=(made, made),
            in_specs=[pl.BlockSpec(memory_space=pltpu.SMEM)] * 3 + [whole] * 6,
            out_specs=(whole, whole),
            scratch_shapes=[
                pltpu.VMEM((blocks, 2, QUARTERS, share // QUARTERS, width), jnp.bfloat16),
                pltpu.VMEM((2, rows, width), jnp.bfloat16),
                pltpu.VMEM((2, 2 * (rows + texts), 2 * width), jnp.bfloat16),
                pltpu.VMEM((2 * rows, width), jnp.bfloat16),
                pltpu.VMEM(gate_table.shape, jnp.float32),
                pltpu.VMEM((2 * rows, features), jnp.bfloat16),
                pltpu.SemaphoreType.DMA((blocks, 2)),
                pltpu.SemaphoreType.DMA((blocks, QUARTERS, 5)),
                pltpu.SemaphoreType.DMA((blocks, QUARTERS)),
                pltpu.SemaphoreType.DMA((blocks, QUARTERS)),
                pltpu.SemaphoreType.DMA((4,)),
                pltpu.SemaphoreType.DMA((4,)),
                pltpu.SemaphoreType.DMA((8,)),
            ],
            compiler_params=pltpu.CompilerParams(
                collective_id=0, has_side_effects=True, vmem_limit_bytes=62 * 1024 * 1024
            ),
        )(
            timesteps,
            image_lengths,
            text_lengths,
            shard,
            image_qkv,
            image_qkv_tangent,
            text_kv,
            text_kv_tangent,
            gate_table,
        )
    )


def fits(mesh):
    sizes = dict(mesh.shape)
    return sizes["grp"] == 2 and sizes["seq"] == 2 and sizes["blk"] == 2 * DEPTH


def solution(mesh):
    in_specs = (
        P(("grp", "blk", "seq"), None),
        P(("grp", "blk", "seq"), None),
        P(("grp", "blk", "seq"), None),
        P(("grp", "blk", "seq"), None),
        P(None, ("blk", "seq")),
        P(),
        P(("grp", "blk")),
        P(("grp", "blk")),
        P(("grp", "blk")),
    )
    out_specs = (P(("grp", "blk", "seq"), None), P(("grp", "blk", "seq"), None))
    chosen = fused_body if fits(mesh) else body
    return jax.shard_map(chosen, mesh=mesh, in_specs=in_specs, out_specs=out_specs, check_vma=False)
```
